128 devices in a mesh: ctx: 8 (over z, core), tp: 16 (over y, x).
Axes of the slice: x: 4, y: 4, z: 4, core: 2. Of those that a mesh axis runs over, the one named last changes fastest.
Arguments:
- tokens: bfloat16 [16384, 4096], P(('ctx', 'tp')), may hold values from -45 to 45, as said below
- norm_gain: float32 [4096], replicated, may hold values from 0.1 to 1.9
- w_in: bfloat16 [4096, 3, 4096], P(None, None, 'tp'), may hold values from -0.09375 to 0.09375
- conv_w: float32 [7, 3, 4096], P(None, None, 'tp'), may hold values from -2.5 to 2.5
- decay_rate: float32 [16, 4096], P(None, 'tp'), may hold values from 1e-06 to 0.15, as said below
- residue: float32 [16, 4096], P(None, 'tp'), may hold values from -0.6 to 0.6, as said below
- skip_gain: float32 [4096], P('tp'), may hold values from -3 to 3
- w_out: bfloat16 [4096, 4096], P('tp'), may hold values from -0.09375 to 0.09375
Outputs:
- block_out: bfloat16 [16384, 4096], P(('ctx', 'tp'))
The draws below stay inside these ranges and needn't reach their ends.
Inputs may be any that keep to these rules, and one draw needn't show every extreme that they name: `tokens`: activations entering the block. `decay_rate`: decay rates are positive. `residue`: residues of the modal filter.
All inputs are finite; a program needn't handle non-finite values.
Results may differ from the reference program's by a relative error of at most 0.024.
Values may be sent and summed in bfloat16 or wider, within the bound.
A program may use at most 192 MiB of HBM per device.

```python
import math
import jax
import jax.numpy as jnp
from jax import lax

D = 4096
POLES = 16
TAPS = 7
BLOCK = 128
CH = 256
SEQ = 16384
N_TP = 16


def draw_tokens(key, part):
    first_key = jax.random.fold_in(key, 101)
    second_key = jax.random.fold_in(key, 102)
    third_key = jax.random.fold_in(key, 103)
    base_draw = jnp.clip(jax.random.normal(first_key, (SEQ, D), jnp.float32), -5.0, 5.0)
    row_scale = jnp.exp(jax.random.uniform(second_key, (SEQ, 1), jnp.float32, math.log(0.3), math.log(3.0)))
    col_scale = jnp.exp(jax.random.uniform(third_key, (1, D), jnp.float32, math.log(0.3), math.log(3.0)))
    return (base_draw * row_scale * col_scale).astype(jnp.bfloat16)


def rate_draw(key):
    first_key = jax.random.fold_in(key, 201)
    lowest = math.log(1e-06)
    wide_rates = jnp.exp(jax.random.uniform(first_key, (POLES, D), jnp.float32, lowest, math.log(0.15)))
    return wide_rates


def draw_decay_rate(key, part):
    return rate_draw(key)


def draw_residue(key, part):
    rates = rate_draw(key)
    noise = jnp.clip(jax.random.normal(jax.random.fold_in(key, 204), (POLES, D), jnp.float32), -4.0, 4.0)
    return noise * jnp.sqrt(2.0 * rates + 2.0 / SEQ) * 0.25


def shard_levels(rng, extent, shards, least, top_value):
    factor_of, own = 1.0, jax.random.fold_in(rng, 6)
    for dim, shards_of in shards:
        steps = jnp.exp(jax.random.uniform(jax.random.fold_in(own, dim), (shards_of,), jnp.float32, least / len(shards), top_value / len(shards)))
        factor_of = factor_of * jnp.repeat(steps, extent[dim] // shards_of).reshape([-1 if axis == dim else 1 for axis in range(len(extent))])
    return factor_of


def centred(own_key, extent, scale, bound, shards=(), kind=jnp.bfloat16):
    entries = jax.random.normal(own_key, extent, jnp.float32) * scale
    if len(shards) > 0:
        entries = shard_levels(own_key, extent, shards, -0.22, 0.18) * entries
    return jnp.clip(entries, min=-bound, max=bound).astype(kind)


def setup_inputs(seed: int = 0) -> dict:
    seeds = jax.random.split(jax.random.key(seed), 9)
    tokens = draw_tokens(jax.random.fold_in(seeds[8], 71), 0)
    norm_gain = jnp.clip(1.0 + 0.18 * jax.random.normal(seeds[1], (D,), jnp.float32), 0.1, 1.9)
    w_in = centred(seeds[2], (D, 3, D), D ** -0.5, 0.09375, ((2, 16),))
    conv_w = centred(seeds[3], (TAPS, 3, D), 0.4, 2.5, ((2, 16),), jnp.float32)
    decay_rate = draw_decay_rate(jax.random.fold_in(seeds[8], 71), 0)
    residue = draw_residue(jax.random.fold_in(seeds[8], 71), 0)
    skip_gain = centred(seeds[6], (D,), 0.5, 3.0, ((0, 16),), jnp.float32)
    w_out = centred(seeds[7], (D, D), D ** -0.5, 0.09375, ((0, 16),))
    return dict(tokens=tokens, norm_gain=norm_gain, w_in=w_in, conv_w=conv_w, decay_rate=decay_rate, residue=residue, skip_gain=skip_gain, w_out=w_out)


epsilon = 1e-05
highest = lax.Precision.HIGHEST

def normalize(tokens, norm_gain):
    floats = tokens.astype(jnp.float32)
    mean_square = lax.optimization_barrier(jnp.mean(floats * floats, axis=1, keepdims=True))
    return (floats * lax.rsqrt(mean_square + epsilon) * norm_gain).astype(jnp.bfloat16)

def featurize(projected, tail_rows, conv_w):
    filter_taps = conv_w.reshape(TAPS, -1)
    extended = jnp.concatenate([tail_rows, projected], axis=-2).astype(jnp.float32)
    length = projected.shape[-2]
    summed = filter_taps[0] * extended[..., 0:length, :]
    for offset in range(1, TAPS):
        summed = summed + filter_taps[offset] * extended[..., offset:offset + length, :]
    return summed

def decay_tables(decay_rate, residue, block):
    distance = jnp.arange(block, dtype=jnp.float32)
    powers = jnp.exp(-decay_rate[None] * distance[:, None, None])
    impulse = lax.optimization_barrier(jnp.sum(powers * residue[None], axis=1))
    positions = jnp.arange(block, dtype=jnp.int32)
    lag_rows = positions[:, None] - positions[None, :]
    toeplitz = jnp.where((lag_rows >= 0)[:, :, None], impulse[jnp.maximum(lag_rows, 0)], 0.0)
    end_power = jnp.exp(-decay_rate[None] * (block - 1.0 - distance)[:, None, None])
    out_power = jnp.exp(-decay_rate[None] * (distance + 1.0)[:, None, None]) * residue[None]
    return (toeplitz, end_power, out_power)

def reference(tokens, norm_gain, w_in, conv_w, decay_rate, residue, skip_gain, w_out):
    toeplitz, end_power, out_power = decay_tables(decay_rate, residue, BLOCK)
    block_decay = jnp.exp(-decay_rate * BLOCK)
    flat_w = w_in.reshape(D, 3 * D)
    w_groups = w_out.reshape(N_TP, CH, D).astype(jnp.float32)
    margin = TAPS - 1

    def advance(carried, block_rows):
        tail_rows, states = carried
        normed = normalize(block_rows, norm_gain)
        projected = jnp.dot(normed, flat_w, preferred_element_type=jnp.float32).astype(jnp.bfloat16)
        features = featurize(projected, tail_rows, conv_w)
        queries = features[:, :D]
        product = features[:, D:2 * D] * features[:, 2 * D:]
        within = jnp.einsum('tsc,sc->tc', toeplitz, product, precision=highest)
        from_state = jnp.einsum('tnc,nc->tc', out_power, states, precision=highest)
        gated = (queries * (within + from_state + skip_gain * product)).astype(jnp.bfloat16)
        partials = jnp.einsum('bgc,gcd->bgd', gated.reshape(BLOCK, N_TP, CH).astype(jnp.float32), w_groups, precision=highest)
        partials = lax.optimization_barrier(partials.astype(jnp.bfloat16)).astype(jnp.float32)
        mixed = lax.optimization_barrier(jnp.sum(partials, axis=1))
        result = (block_rows.astype(jnp.float32) + mixed).astype(jnp.bfloat16)
        block_ends = jnp.einsum('sc,snc->nc', product, end_power, precision=highest)
        return ((projected[BLOCK - margin:], block_decay * states + block_ends), result)
    initial = (jnp.zeros((margin, 3 * D), jnp.bfloat16), jnp.zeros((POLES, D), jnp.float32))
    _, results = lax.scan(advance, initial, tokens.reshape(SEQ // BLOCK, BLOCK, D))
    return results.reshape(SEQ, D)
```

```python
import functools

import jax
import jax.numpy as jnp
from jax import lax
from jax.experimental import pallas as pl
from jax.experimental.pallas import tpu as pltpu
from jax.sharding import PartitionSpec as P

TAPS = 7
POLES = 16
D = 4096
CH = 256
ROWS = 128
TEAM = 512
HALO = 16
SEGS = 8
STEPS = TEAM // SEGS
LEAD = 8
EPS = 1e-05
MESH = pl.DeviceIdType.MESH
NSEM = 96
OUT_COLS = 512
OUT_PARTS = D // OUT_COLS

f32 = jnp.float32
bf16 = jnp.bfloat16


def tree_sum(parts):
    parts = list(parts)
    while len(parts) > 1:
        parts = [
            parts[i] + parts[i + 1] if i + 1 < len(parts) else parts[i]
            for i in range(0, len(parts), 2)
        ]
    return parts[0]


def kernel(
    tok_h, gain, win_h, conv, decay, res, skip, wout_h,
    out_h,
    tok, lhs, w_all, w_out, par, proj, prod, q_all, y_all, pref, gbuf, gated,
    stage, landed, ends, totals, carry, outv, send, recv, osend, orecv, local,
):
    ctx = lax.axis_index("ctx")
    tp = lax.axis_index("tp")
    z, k = ctx // 2, ctx % 2
    y, x = tp // 4, tp % 4

    def dev(dz=0, dk=0, dy=0, dx=0):
        return (
            ((z + dz) % 4) * 2 + (k + dk) % 2,
            ((y + dy) % 4) * 4 + (x + dx) % 4,
        )

    place = ctx * 4 + y
    after, before = (place + 1) % 32, (place + 31) % 32
    dev_after = (after // 4, (after % 4) * 4 + x)
    dev_before = (before // 4, (before % 4) * 4 + x)

    count = [0]
    started = []

    def remote(src, dst, device):
        i = count[0]
        count[0] += 1
        return pltpu.make_async_remote_copy(
            src_ref=src, dst_ref=dst, send_sem=send.at[i], recv_sem=recv.at[i],
            device_id=device, device_id_type=MESH,
        )

    def go(copy):
        copy.start()
        started.append(copy)
        return copy

    gm, gp, g2 = (y + 3) % 4, (y + 1) % 4, (y + 2) % 4

    copy_tok = pltpu.make_async_copy(tok_h, tok, local.at[0])
    copy_win = pltpu.make_async_copy(win_h, w_all.at[y], local.at[1])
    copy_out = pltpu.make_async_copy(
        wout_h, w_out.at[pl.ds(pl.multiple_of(y * CH, CH), CH)], local.at[2]
    )
    copy_tok.start()
    copy_win.start()
    copy_out.start()

    for s in range(3):
        par[y, s * 8:s * 8 + TAPS, :] = conv[s]
    par[y, 24:40, :] = decay[...]
    par[y, 40:56, :] = res[...]
    par[y, 56:57, :] = skip[...]

    partners = [dev(dx=1), dev(dx=2), dev(dx=3), dev(dy=1), dev(dy=2), dev(dy=3)]
    partners += [dev(dz=a, dk=b) for a in range(4) for b in range(2) if a or b]
    partners += [dev_after, dev_before]
    barrier = pltpu.get_barrier_semaphore()
    for d in partners:
        pl.semaphore_signal(barrier, inc=1, device_id=d, device_id_type=MESH)
    pl.semaphore_wait(barrier, len(partners))

    YP, YM, ZP, ZM, SIB = dev(dy=1), dev(dy=3), dev(dz=1), dev(dz=3), dev(dk=1)
    XP, XM = dev(dx=1), dev(dx=3)

    def rows_in(zz, n=512):
        return pl.ds(pl.multiple_of(k * 2048 + zz * n, n), n)

    def piece(kind, g, zz, half):
        if kind == "in":
            return w_all.at[g, 1 + half, rows_in(zz)]
        at = g * CH + k * 128 + zz * 32 + half * 16
        return w_out.at[pl.ds(pl.multiple_of(at, 16), 16)]

    def own_piece(kind, half):
        if kind == "in":
            return win_h.at[1 + half, rows_in(z)]
        at = k * 128 + z * 32 + half * 16
        return wout_h.at[pl.ds(pl.multiple_of(at, 16), 16)]

    class Weights:
        def __init__(self, kind):
            self.kind = kind
            own = lambda h, d: remote(own_piece(kind, h), piece(kind, y, z, h), d)
            self.to_p = [own(h, YP) for h in range(2)]
            self.to_m = [own(h, YM) for h in range(2)]
            self.fwd_p = remote(piece(kind, gm, z, 0), piece(kind, gm, z, 0), YP)
            self.fwd_m = remote(piece(kind, gp, z, 1), piece(kind, gp, z, 1), YM)
            same = lambda g, zz, h, d: remote(piece(kind, g, zz, h), piece(kind, g, zz, h), d)
            self.z_p, self.z_m, self.zf_p, self.zf_m = {}, {}, {}, {}
            for name, g in (("m", gm), ("p", gp), ("2", g2)):
                self.z_p[name] = [same(g, z, h, ZP) for h in range(2)]
                self.z_m[name] = [same(g, z, h, ZM) for h in range(2)]
                self.zf_p[name] = same(g, (z + 3) % 4, 0, ZP)
                self.zf_m[name] = same(g, (z + 1) % 4, 1, ZM)

        def start(self):
            for h in (0, 1):
                go(self.to_p[h] if h == 0 else self.to_m[h])
                go(self.to_m[h] if h == 0 else self.to_p[h])

        def spread(self, name, h):
            go(self.z_p[name][h])
            go(self.z_m[name][h])

        def along_y(self):
            self.to_p[0].wait_recv()
            go(self.fwd_p)
            self.spread("m", 0)
            self.to_m[0].wait_recv()
            self.spread("p", 0)
            self.to_m[1].wait_recv()
            go(self.fwd_m)
            self.spread("p", 1)
            self.to_p[1].wait_recv()
            self.spread("m", 1)

        def along_y2(self):
            self.fwd_p.wait_recv()
            self.spread("2", 0)
            self.fwd_m.wait_recv()
            self.spread("2", 1)

        def forward_z(self, name):
            self.z_p[name][0].wait_recv()
            go(self.zf_p[name])
            self.z_m[name][1].wait_recv()
            go(self.zf_m[name])

        def finish(self, name):
            self.z_m[name][0].wait_recv()
            self.z_p[name][1].wait_recv()
            self.zf_p[name].wait_recv()
            self.zf_m[name].wait_recv()

    wi = Weights("in")
    wo = Weights("out")

    def q_rows(h):
        return pl.ds(pl.multiple_of(k * 2048 + h * 1024, 1024), 1024)

    def q_own(h, d):
        return remote(win_h.at[0, q_rows(h)], w_all.at[y, 0, q_rows(h)], d)

    q_p = [q_own(h, YP) for h in range(2)]
    q_m = [q_own(h, YM) for h in range(2)]
    q_fp = remote(w_all.at[gm, 0, q_rows(0)], w_all.at[gm, 0, q_rows(0)], YP)
    q_fm = remote(w_all.at[gp, 0, q_rows(1)], w_all.at[gp, 0, q_rows(1)], YM)

    half = pl.ds(pl.multiple_of(k * 2048, 2048), 2048)
    push = {}
    push_out = {}
    for name, g in (("m", gm), ("p", gp), ("2", g2)):
        push[name] = [remote(w_all.at[g, s, half], w_all.at[g, s, half], SIB) for s in range(3)]
        o_half = pl.ds(pl.multiple_of(g * CH + k * 128, 128), 128)
        push_out[name] = remote(w_out.at[o_half], w_out.at[o_half], SIB)

    par_copies = [remote(par.at[y], par.at[y], dev(dy=d)) for d in (1, 3, 2)]

    def x_rows(who, h):
        return lhs.at[pl.ds(pl.multiple_of(HALO + who * ROWS + h * 64, 16), 64)]

    x_p = [remote(x_rows(x, h), x_rows(x, h), XP) for h in range(2)]
    x_m = [remote(x_rows(x, h), x_rows(x, h), XM) for h in range(2)]
    xm, xp = (x + 3) % 4, (x + 1) % 4
    x_fp = remote(x_rows(xm, 0), x_rows(xm, 0), XP)
    x_fm = remote(x_rows(xp, 1), x_rows(xp, 1), XM)
    halo_copy = remote(lhs.at[pl.ds(TEAM, HALO)], lhs.at[pl.ds(0, HALO)], dev_after)

    wi.start()
    copy_tok.wait()

    def norm_rows(i, c):
        v = tok[pl.ds(pl.multiple_of(i * 16, 16), 16), :].astype(f32)
        ms = jnp.sum(v * v, axis=1, keepdims=True) * (1.0 / D)
        v = (v * lax.rsqrt(ms + EPS) * gain[...]).astype(bf16)
        lhs[pl.ds(pl.multiple_of(HALO + x * ROWS + i * 16, 16), 16), :] = v
        return c

    lax.fori_loop(0, 4, norm_rows, 0)
    go(x_p[0])
    go(x_m[0])
    lax.fori_loop(4, 8, norm_rows, 0)
    go(x_m[1])
    go(x_p[1])
    for c in par_copies:
        go(c)
    go(q_p[0])
    go(q_m[1])
    go(q_m[0])
    go(q_p[1])

    wi.along_y()
    wi.along_y2()
    x_p[0].wait_recv()
    go(x_fp)
    x_m[1].wait_recv()
    go(x_fm)
    wi.forward_z("m")
    wi.forward_z("p")
    q_p[0].wait_recv()
    go(q_fp)
    q_m[1].wait_recv()
    go(q_fm)
    wo.start()
    x_p[1].wait_recv()
    x_m[0].wait_recv()
    x_fp.wait_recv()
    x_fm.wait_recv()
    go(halo_copy)
    for c in par_copies:
        c.wait_recv()
    copy_win.wait()
    halo_copy.wait_recv()

    @pl.when(place == 0)
    def _():
        lhs[0:HALO, :] = jnp.zeros((HALO, D), bf16)

    sub = lax.broadcasted_iota(jnp.int32, (SEGS, 128), 0)

    def project(g):
        for s in range(3):
            def k_step(j, acc):
                at = pl.ds(pl.multiple_of(j * 1024, 1024), 1024)
                return acc + jnp.dot(lhs[:, at], w_all[g, s, at, :], preferred_element_type=f32)

            acc = lax.fori_loop(0, 4, k_step, jnp.zeros((HALO + TEAM, CH), f32))
            acc = acc.astype(bf16).astype(f32)
            for h in range(2):
                part = acc[:, h * 128:(h + 1) * 128]
                for seg in range(SEGS):
                    proj[s, h, pl.ds(LEAD * SEGS + seg, STEPS, stride=SEGS), :] = part[
                        HALO + seg * STEPS:HALO + (seg + 1) * STEPS
                    ]
                for j in range(1, TAPS):
                    last = proj[s, h, pl.ds((LEAD + STEPS - j) * SEGS, SEGS), :]
                    first = jnp.broadcast_to(part[HALO - j:HALO - j + 1], (SEGS, 128))
                    proj[s, h, pl.ds((LEAD - j) * SEGS, SEGS), :] = jnp.where(
                        sub == 0, first, pltpu.roll(last, 1, 0)
                    )

    def featurize(g):
        for h in range(2):
            lanes = pl.ds(h * 128, 128)
            taps = [par[g, s * 8:s * 8 + 8, lanes] for s in range(3)]

            def steps(i, c):
                feats = []
                for s in range(3):
                    at = pl.multiple_of((i * 8 + LEAD - TAPS + 1) * SEGS, SEGS)
                    rows = proj[s, h, pl.ds(at, 14 * SEGS), :]
                    feats.append(tree_sum([
                        taps[s][j:j + 1] * rows[j * SEGS:j * SEGS + 64] for j in range(TAPS)
                    ]))
                to = pl.ds(pl.multiple_of(i * 64, 64), 64)
                q_all[g, h, to, :] = feats[0]
                prod[h, to, :] = feats[1] * feats[2]
                return c

            lax.fori_loop(0, STEPS // 8, steps, 0)

    def scan(g):
        for h in range(2):
            lanes = pl.ds(h * 128, 128)
            rate = par[g, 24:40, lanes]
            rs = par[g, 40:56, lanes]
            wide = lambda v: jnp.broadcast_to(v, (SEGS, 128))
            power = jnp.exp(-rate)
            a = [wide(power[n:n + 1]) for n in range(POLES)]
            r = [wide(rs[n:n + 1]) for n in range(POLES)]
            direct = wide(par[g, 56:57, lanes])

            def steps(i, states):
                for u in range(4):
                    at = pl.ds(pl.multiple_of((i * 4 + u) * SEGS, SEGS), SEGS)
                    v = prod[h, at, :]
                    states = [a[n] * states[n] + r[n] * v for n in range(POLES)]
                    y_all[g, h, at, :] = tree_sum(states) + direct * v
                return states

            states = lax.fori_loop(
                0, STEPS // 4, steps, [jnp.zeros((SEGS, 128), f32)] * POLES
            )
            for n in range(POLES):
                v = states[n]
                for dist in (1, 2, 4):
                    hop = jnp.exp(rate[n:n + 1] * (-1.0 * STEPS * dist))
                    v = v + hop * jnp.where(sub >= dist, pltpu.roll(v, dist, 0), 0.0)
                pref[g, h, n] = jnp.where(sub >= 1, pltpu.roll(v, 1, 0), 0.0)
                ends[y, g, h, n:n + 1, :] = v[SEGS - 1:SEGS]

    def weights_ready(name):
        wi.finish(name)
        go(push[name][1])
        go(push[name][2])

    def q_ready(name):
        if name == "m":
            q_p[1].wait_recv()
        elif name == "p":
            q_m[0].wait_recv()
        else:
            q_fp.wait_recv()
            q_fm.wait_recv()
        go(push[name][0])

    def group(i, c):
        @pl.when(i == 1)
        def _():
            wi.forward_z("2")
            q_ready("m")
            q_ready("p")
            weights_ready("m")
            wo.along_y()
            weights_ready("p")
            for c in push["m"]:
                c.wait_recv()

        @pl.when(i == 2)
        def _():
            wo.along_y2()
            q_ready("2")
            for c in push["p"]:
                c.wait_recv()

        @pl.when(i == 3)
        def _():
            weights_ready("2")
            wo.forward_z("m")
            wo.forward_z("p")
            for c in push["2"]:
                c.wait_recv()

        turn = jnp.where(i == 0, 0, jnp.where(i == 1, 3, jnp.where(i == 2, 1, 2)))
        g = (y + turn) % 4
        project(g)
        featurize(g)
        scan(g)
        return c

    lax.fori_loop(0, 4, group, 0)

    end_copies = [remote(ends.at[y], ends.at[y], dev(dy=d)) for d in (1, 3, 2)]
    for c in end_copies:
        go(c)
    wo.forward_z("2")
    for c in end_copies:
        c.wait_recv()
    for g in range(4):
        for h in range(2):
            rate = par[g, 24:40, h * 128:(h + 1) * 128]
            hop = jnp.exp(rate * (-1.0 * TEAM))
            total = ends[0, g, h]
            for yy in range(1, 4):
                total = hop * total + ends[yy, g, h]
            totals[ctx, g, h] = total
    total_copies = [
        remote(totals.at[ctx], totals.at[ctx], dev(dz=a, dk=b))
        for a in range(4) for b in range(2) if a or b
    ]
    for c in total_copies:
        go(c)
    for name in ("m", "p", "2"):
        wo.finish(name)
        go(push_out[name])
    for c in total_copies:
        c.wait_recv()

    for g in range(4):
        for h in range(2):
            rate = par[g, 24:40, h * 128:(h + 1) * 128]
            far = jnp.exp(rate * (-4.0 * TEAM))
            near = jnp.exp(rate * (-1.0 * TEAM))
            v = jnp.zeros((POLES, 128), f32)
            for cc in range(7):
                v = jnp.where(cc < ctx, far * v + totals[cc, g, h], v)
            for yy in range(3):
                v = jnp.where(yy < y, near * v + ends[yy, g, h], v)
            carry[g, h] = v

    segs = sub.astype(f32)

    def correct(g, c):
        for h in range(2):
            lanes = pl.ds(h * 128, 128)
            rate = par[g, 24:40, lanes]
            power = jnp.exp(-rate)
            wide = lambda v: jnp.broadcast_to(v, (SEGS, 128))
            a = [wide(power[n:n + 1]) for n in range(POLES)]
            begin = carry[g, h]
            states = []
            for n in range(POLES):
                seg_power = jnp.exp(wide(rate[n:n + 1]) * (segs * (-1.0 * STEPS)))
                states.append(pref[g, h, n] + seg_power * wide(begin[n:n + 1]))

            def steps(i, states):
                for u in range(4):
                    at = pl.ds(pl.multiple_of((i * 4 + u) * SEGS, SEGS), SEGS)
                    states = [a[n] * states[n] for n in range(POLES)]
                    gbuf[h, at, :] = q_all[g, h, at, :] * (y_all[g, h, at, :] + tree_sum(states))
                return states

            lax.fori_loop(0, STEPS // 4, steps, states)
            for seg in range(SEGS):
                gated[g, seg * STEPS:(seg + 1) * STEPS, h * 128:(h + 1) * 128] = gbuf[
                    h, pl.ds(seg, STEPS, stride=SEGS), :
                ].astype(bf16)
        return c

    lax.fori_loop(0, 4, correct, 0)

    copy_out.wait()
    for name in ("m", "p", "2"):
        push_out[name].wait_recv()

    def part_copy(n, d):
        cols = pl.ds(pl.multiple_of(n * OUT_COLS, OUT_COLS), OUT_COLS)
        to = (x + d) % 4
        rows = pl.ds(pl.multiple_of(to * ROWS, ROWS), ROWS)
        return pltpu.make_async_remote_copy(
            src_ref=stage.at[rows, cols], dst_ref=landed.at[x, :, cols],
            send_sem=osend.at[d - 1, n], recv_sem=orecv.at[d - 1, n],
            device_id=dev(dx=d), device_id_type=MESH,
        )

    def out_part(n, c):
        cols = pl.ds(pl.multiple_of(n * OUT_COLS, OUT_COLS), OUT_COLS)
        acc = jnp.zeros((TEAM, OUT_COLS), f32)
        for g in range(4):
            acc = acc + jnp.dot(gated[g], w_out[g * CH:(g + 1) * CH, cols], preferred_element_type=f32)
        stage[:, cols] = acc.astype(bf16)
        for d in (2, 1, 3):
            part_copy(n, d).start()
        return c

    lax.fori_loop(0, OUT_PARTS, out_part, 0)

    def add_part(n, c):
        cols = pl.ds(pl.multiple_of(n * OUT_COLS, OUT_COLS), OUT_COLS)
        for d in (1, 2, 3):
            part_copy(n, d).wait_recv()
        total = tok[:, cols].astype(f32) + stage[
            pl.ds(pl.multiple_of(x * ROWS, ROWS), ROWS), cols
        ].astype(f32)
        for d in (1, 2, 3):
            total = total + landed[(x + d) % 4, :, cols].astype(f32)
        outv[:, cols] = total.astype(bf16)
        return c

    lax.fori_loop(0, OUT_PARTS, add_part, 0)
    copy_res = pltpu.make_async_copy(outv, out_h, local.at[3])
    copy_res.start()

    def sent_part(n, c):
        for d in (1, 2, 3):
            part_copy(n, d).wait_send()
        return c

    lax.fori_loop(0, OUT_PARTS, sent_part, 0)
    for c in started:
        c.wait_send()
    copy_res.wait()


def shards(tokens, norm_gain, w_in, conv_w, decay_rate, residue, skip_gain, w_out):
    anywhere = pl.BlockSpec(memory_space=pl.ANY)
    inside = pl.BlockSpec(memory_space=pltpu.VMEM)
    vmem = pltpu.VMEM
    return pl.pallas_call(
        kernel,
        out_shape=jax.ShapeDtypeStruct(tokens.shape, tokens.dtype),
        in_specs=[anywhere, inside, anywhere, inside, inside, inside, inside, anywhere],
        out_specs=anywhere,
        scratch_shapes=[
            vmem((ROWS, D), bf16),
            vmem((HALO + TEAM, D), bf16),
            vmem((4, 3, D, CH), bf16),
            vmem((4 * CH, D), bf16),
            vmem((4, 64, CH), f32),
            vmem((3, 2, (LEAD + STEPS) * SEGS, 128), f32),
            vmem((2, TEAM, 128), f32),
            vmem((4, 2, TEAM, 128), f32),
            vmem((4, 2, TEAM, 128), f32),
            vmem((4, 2, POLES, SEGS, 128), f32),
            vmem((2, TEAM, 128), f32),
            vmem((4, TEAM, CH), bf16),
            vmem((TEAM, D), bf16),
            vmem((4, ROWS, D), bf16),
            vmem((4, 4, 2, POLES, 128), f32),
            vmem((8, 4, 2, POLES, 128), f32),
            vmem((4, 2, POLES, 128), f32),
            vmem((ROWS, D), bf16),
            pltpu.SemaphoreType.DMA((NSEM,)),
            pltpu.SemaphoreType.DMA((NSEM,)),
            pltpu.SemaphoreType.DMA((3, OUT_PARTS)),
            pltpu.SemaphoreType.DMA((3, OUT_PARTS)),
            pltpu.SemaphoreType.DMA((4,)),
        ],
        compiler_params=pltpu.CompilerParams(
            collective_id=0, has_side_effects=True, vmem_limit_bytes=62 * 1024 * 1024
        ),
    )(
        tokens,
        norm_gain.reshape(1, D),
        jnp.transpose(w_in, (1, 0, 2)),
        jnp.transpose(conv_w, (1, 0, 2)),
        decay_rate,
        residue,
        skip_gain.reshape(1, CH),
        w_out,
    )


def solution(mesh):
    return jax.shard_map(
        shards,
        mesh=mesh,
        in_specs=(
            P(("ctx", "tp"), None),
            P(),
            P(None, None, "tp"),
            P(None, None, "tp"),
            P(None, "tp"),
            P(None, "tp"),
            P("tp"),
            P("tp", None),
        ),
        out_specs=P(("ctx", "tp"), None),
        check_vma=False,
    )
```

```python
import functools

import jax
import jax.numpy as jnp
from jax import lax
from jax.experimental import pallas as pl
from jax.experimental.pallas import tpu as pltpu
from jax.sharding import PartitionSpec as P

TAPS = 7
POLES = 16
D = 4096
CH = 256
ROWS = 128
TEAM = 512
HALO = 16
SEGS = 8
STEPS = TEAM // SEGS
LEAD = 8
EPS = 1e-05
MESH = pl.DeviceIdType.MESH
NSEM = 150
OUT_COLS = 512
OUT_PARTS = D // OUT_COLS
HALF_COLS = D // 2

f32 = jnp.float32
bf16 = jnp.bfloat16


def tree_sum(parts):
    parts = list(parts)
    while len(parts) > 1:
        parts = [
            parts[i] + parts[i + 1] if i + 1 < len(parts) else parts[i]
            for i in range(0, len(parts), 2)
        ]
    return parts[0]


def kernel(
    tok_h, gain, win_h, conv, decay, res, skip, wout_h,
    out_h,
    tok, lhs, w_all, w_out, par, proj, prod, q_all, y_all, pref, gbuf, gated,
    stage, far, near, ends, totals, carry, outv, send, recv, osend, orecv, local,
):
    ctx = lax.axis_index("ctx")
    tp = lax.axis_index("tp")
    z, k = ctx // 2, ctx % 2
    y, x = tp // 4, tp % 4

    def dev(dz=0, dk=0, dy=0, dx=0):
        return (
            ((z + dz) % 4) * 2 + (k + dk) % 2,
            ((y + dy) % 4) * 4 + (x + dx) % 4,
        )

    place = ctx * 4 + y
    after, before = (place + 1) % 32, (place + 31) % 32
    dev_after = (after // 4, (after % 4) * 4 + x)
    dev_before = (before // 4, (before % 4) * 4 + x)

    count = [0]
    started = []

    def remote(src, dst, device):
        i = count[0]
        count[0] += 1
        return pltpu.make_async_remote_copy(
            src_ref=src, dst_ref=dst, send_sem=send.at[i], recv_sem=recv.at[i],
            device_id=device, device_id_type=MESH,
        )

    def go(copy):
        copy.start()
        started.append(copy)
        return copy

    gm, gp, g2 = (y + 3) % 4, (y + 1) % 4, (y + 2) % 4

    copy_tok = pltpu.make_async_copy(tok_h, tok, local.at[0])
    copy_win = pltpu.make_async_copy(win_h, w_all.at[y], local.at[1])
    copy_out = pltpu.make_async_copy(
        wout_h, w_out.at[pl.ds(pl.multiple_of(y * CH, CH), CH)], local.at[2]
    )
    copy_tok.start()
    copy_win.start()
    copy_out.start()

    for s in range(3):
        par[y, s * 8:s * 8 + TAPS, :] = conv[s]
    par[y, 24:40, :] = decay[...]
    par[y, 40:56, :] = res[...]
    par[y, 56:57, :] = skip[...]

    partners = [dev(dx=1), dev(dx=2), dev(dx=3), dev(dy=1), dev(dy=2), dev(dy=3)]
    partners += [dev(dz=a, dk=b) for a in range(4) for b in range(2) if a or b]
    partners += [dev_after, dev_before]
    barrier = pltpu.get_barrier_semaphore()
    for d in partners:
        pl.semaphore_signal(barrier, inc=1, device_id=d, device_id_type=MESH)
    pl.semaphore_wait(barrier, len(partners))

    YP, YM, ZP, ZM, SIB = dev(dy=1), dev(dy=3), dev(dz=1), dev(dz=3), dev(dk=1)
    XP, XM = dev(dx=1), dev(dx=3)

    def rows_in(zz, n=512):
        return pl.ds(pl.multiple_of(k * 2048 + zz * n, n), n)

    def piece(kind, g, zz, half):
        if kind == "in":
            return w_all.at[g, 1 + half, rows_in(zz)]
        at = g * CH + k * 128 + zz * 32 + half * 16
        return w_out.at[pl.ds(pl.multiple_of(at, 16), 16), pl.ds(kind * HALF_COLS, HALF_COLS)]

    def own_piece(kind, half):
        if kind == "in":
            return win_h.at[1 + half, rows_in(z)]
        at = k * 128 + z * 32 + half * 16
        return wout_h.at[pl.ds(pl.multiple_of(at, 16), 16), pl.ds(kind * HALF_COLS, HALF_COLS)]

    class Weights:
        def __init__(self, kind):
            self.kind = kind
            own = lambda h, d: remote(own_piece(kind, h), piece(kind, y, z, h), d)
            self.to_p = [own(h, YP) for h in range(2)]
            self.to_m = [own(h, YM) for h in range(2)]
            self.fwd_p = remote(piece(kind, gm, z, 0), piece(kind, gm, z, 0), YP)
            self.fwd_m = remote(piece(kind, gp, z, 1), piece(kind, gp, z, 1), YM)
            same = lambda g, zz, h, d: remote(piece(kind, g, zz, h), piece(kind, g, zz, h), d)
            self.z_p, self.z_m, self.zf_p, self.zf_m, self.push = {}, {}, {}, {}, {}
            for name, g in (("m", gm), ("p", gp), ("2", g2)):
                self.z_p[name] = [same(g, z, h, ZP) for h in range(2)]
                self.z_m[name] = [same(g, z, h, ZM) for h in range(2)]
                self.zf_p[name] = same(g, (z + 3) % 4, 0, ZP)
                self.zf_m[name] = same(g, (z + 1) % 4, 1, ZM)
                self.push[name] = {}
                if kind == "in":
                    for dz in range(4):
                        for h in range(2):
                            self.push[name][dz, h] = same(g, (z + dz) % 4, h, SIB)

        def start(self):
            go(self.to_p[0])
            go(self.to_m[1])
            go(self.to_p[1])
            go(self.to_m[0])

        def share(self, name, dz, h):
            if self.kind == "in":
                go(self.push[name][dz, h])

        def spread(self, name, h):
            go(self.z_p[name][h])
            go(self.z_m[name][h])
            self.share(name, 0, h)

        def along_y(self):
            self.to_p[0].wait_recv()
            go(self.fwd_p)
            self.spread("m", 0)
            self.to_m[1].wait_recv()
            go(self.fwd_m)
            self.spread("p", 1)
            self.to_p[1].wait_recv()
            self.spread("m", 1)
            self.to_m[0].wait_recv()
            self.spread("p", 0)

        def along_y2(self):
            self.fwd_p.wait_recv()
            self.spread("2", 0)
            self.fwd_m.wait_recv()
            self.spread("2", 1)

        def forward_p(self, name):
            self.z_p[name][0].wait_recv()
            go(self.zf_p[name])
            self.share(name, 3, 0)

        def forward_m(self, name):
            self.z_m[name][1].wait_recv()
            go(self.zf_m[name])
            self.share(name, 1, 1)

        def forward_z(self):
            self.forward_p("m")
            self.forward_m("p")
            self.forward_m("m")
            self.forward_p("p")

        def finish_near(self, name):
            self.z_m[name][0].wait_recv()
            self.share(name, 1, 0)
            self.z_p[name][1].wait_recv()
            self.share(name, 3, 1)

        def finish_far(self, name):
            self.zf_p[name].wait_recv()
            self.share(name, 2, 0)
            self.zf_m[name].wait_recv()
            self.share(name, 2, 1)

        def finish(self, name):
            self.finish_near(name)
            self.finish_far(name)

    wi = Weights("in")
    wo = [Weights(0), Weights(1)]

    def q_rows(h):
        return pl.ds(pl.multiple_of(k * 2048 + h * 1024, 1024), 1024)

    def q_own(h, d):
        return remote(win_h.at[0, q_rows(h)], w_all.at[y, 0, q_rows(h)], d)

    q_p = [q_own(h, YP) for h in range(2)]
    q_m = [q_own(h, YM) for h in range(2)]
    q_fp = remote(w_all.at[gm, 0, q_rows(0)], w_all.at[gm, 0, q_rows(0)], YP)
    q_fm = remote(w_all.at[gp, 0, q_rows(1)], w_all.at[gp, 0, q_rows(1)], YM)

    q_push = {}
    push_out = {}
    for name, g in (("m", gm), ("p", gp), ("2", g2)):
        q_push[name] = []
        for h in range(2):
            block = w_all.at[g, 0, q_rows(h)]
            q_push[name].append(remote(block, block, SIB))
        o_half = pl.ds(pl.multiple_of(g * CH + k * 128, 128), 128)
        push_out[name] = []
        for c in range(2):
            block = w_out.at[o_half, pl.ds(c * HALF_COLS, HALF_COLS)]
            push_out[name].append(remote(block, block, SIB))

    par_copies = [remote(par.at[y], par.at[y], dev(dy=d)) for d in (1, 3, 2)]

    def x_rows(who, h):
        return lhs.at[pl.ds(pl.multiple_of(HALO + who * ROWS + h * 64, 16), 64)]

    x_p = [remote(x_rows(x, h), x_rows(x, h), XP) for h in range(2)]
    x_m = [remote(x_rows(x, h), x_rows(x, h), XM) for h in range(2)]
    xm, xp = (x + 3) % 4, (x + 1) % 4
    x_fp = remote(x_rows(xm, 0), x_rows(xm, 0), XP)
    x_fm = remote(x_rows(xp, 1), x_rows(xp, 1), XM)
    halo_copy = remote(lhs.at[pl.ds(TEAM, HALO)], lhs.at[pl.ds(0, HALO)], dev_after)

    wi.start()
    copy_tok.wait()

    def norm_rows(i, c):
        v = tok[pl.ds(pl.multiple_of(i * 16, 16), 16), :].astype(f32)
        ms = jnp.sum(v * v, axis=1, keepdims=True) * (1.0 / D)
        v = (v * lax.rsqrt(ms + EPS) * gain[...]).astype(bf16)
        lhs[pl.ds(pl.multiple_of(HALO + x * ROWS + i * 16, 16), 16), :] = v
        return c

    lax.fori_loop(0, 4, norm_rows, 0)
    go(x_p[0])
    lax.fori_loop(4, 8, norm_rows, 0)
    go(x_m[1])
    go(x_p[1])
    go(x_m[0])

    wi.along_y()
    go(q_p[0])
    go(q_m[1])
    go(q_m[0])
    go(q_p[1])
    x_p[0].wait_recv()
    go(x_fp)
    x_m[1].wait_recv()
    go(x_fm)
    wi.forward_p("m")
    wi.forward_m("p")
    for c in par_copies:
        go(c)
    wi.forward_m("m")
    wi.forward_p("p")
    wi.along_y2()
    q_p[0].wait_recv()
    go(q_fp)
    go(q_push["m"][0])
    q_m[1].wait_recv()
    go(q_fm)
    go(q_push["p"][1])
    wi.finish_near("m")
    wi.finish_near("p")
    x_p[1].wait_recv()
    x_m[0].wait_recv()
    x_fp.wait_recv()
    x_fm.wait_recv()
    go(halo_copy)
    copy_win.wait()
    halo_copy.wait_recv()

    @pl.when(place == 0)
    def _():
        lhs[0:HALO, :] = jnp.zeros((HALO, D), bf16)

    sub = lax.broadcasted_iota(jnp.int32, (SEGS, 128), 0)

    def project(g):
        for s in range(3):
            acc = jnp.dot(lhs[...], w_all[g, s], preferred_element_type=f32)
            acc = acc.astype(bf16).astype(f32)
            for h in range(2):
                part = acc[:, h * 128:(h + 1) * 128]
                for seg in range(SEGS):
                    proj[s, h, pl.ds(LEAD * SEGS + seg, STEPS, stride=SEGS), :] = part[
                        HALO + seg * STEPS:HALO + (seg + 1) * STEPS
                    ]
                for j in range(1, TAPS):
                    last = proj[s, h, pl.ds((LEAD + STEPS - j) * SEGS, SEGS), :]
                    first = jnp.broadcast_to(part[HALO - j:HALO - j + 1], (SEGS, 128))
                    proj[s, h, pl.ds((LEAD - j) * SEGS, SEGS), :] = jnp.where(
                        sub == 0, first, pltpu.roll(last, 1, 0)
                    )

    def featurize(g):
        for h in range(2):
            lanes = pl.ds(h * 128, 128)
            taps = [par[g, s * 8:s * 8 + 8, lanes] for s in range(3)]

            def steps(i, c):
                feats = []
                for s in range(3):
                    at = pl.multiple_of((i * 8 + LEAD - TAPS + 1) * SEGS, SEGS)
                    rows = proj[s, h, pl.ds(at, 14 * SEGS), :]
                    feats.append(tree_sum([
                        taps[s][j:j + 1] * rows[j * SEGS:j * SEGS + 64] for j in range(TAPS)
                    ]))
                to = pl.ds(pl.multiple_of(i * 64, 64), 64)
                q_all[g, h, to, :] = feats[0]
                prod[h, to, :] = feats[1] * feats[2]
                return c

            lax.fori_loop(0, STEPS // 8, steps, 0)

    def scan(g):
        for h in range(2):
            lanes = pl.ds(h * 128, 128)
            rate = par[g, 24:40, lanes]
            rs = par[g, 40:56, lanes]
            wide = lambda v: jnp.broadcast_to(v, (SEGS, 128))
            power = jnp.exp(-rate)
            a = [wide(power[n:n + 1]) for n in range(POLES)]
            r = [wide(rs[n:n + 1]) for n in range(POLES)]
            direct = wide(par[g, 56:57, lanes])

            def steps(i, states):
                for u in range(4):
                    at = pl.ds(pl.multiple_of((i * 4 + u) * SEGS, SEGS), SEGS)
                    v = prod[h, at, :]
                    states = [a[n] * states[n] + r[n] * v for n in range(POLES)]
                    y_all[g, h, at, :] = tree_sum(states) + direct * v
                return states

            states = lax.fori_loop(
                0, STEPS // 4, steps, [jnp.zeros((SEGS, 128), f32)] * POLES
            )
            last_rows = []
            for n in range(POLES):
                v = states[n]
                for dist in (1, 2, 4):
                    hop = jnp.exp(rate[n:n + 1] * (-1.0 * STEPS * dist))
                    v = v + hop * jnp.where(sub >= dist, pltpu.roll(v, dist, 0), 0.0)
                pref[g, h, n] = jnp.where(sub >= 1, pltpu.roll(v, 1, 0), 0.0)
                last_rows.append(v[SEGS - 1:SEGS])
            ends[y, g, h] = jnp.concatenate(last_rows, axis=0).astype(bf16)

    def shared(name):
        for c in list(wi.push[name].values()) + q_push[name]:
            c.wait_recv()

    def group(i, c):
        @pl.when(i == 1)
        def _():
            for c in par_copies:
                c.wait_recv()
            shared("m")

        @pl.when(i == 2)
        def _():
            shared("p")

        @pl.when(i == 3)
        def _():
            shared("2")

        turn = jnp.where(i == 0, 0, jnp.where(i == 1, 3, jnp.where(i == 2, 1, 2)))
        g = (y + turn) % 4
        project(g)

        @pl.when(i == 0)
        def _():
            wi.forward_p("2")
            wi.forward_m("2")
            wi.finish_far("m")
            q_p[1].wait_recv()
            go(q_push["m"][1])
            q_m[0].wait_recv()
            go(q_push["p"][0])

        @pl.when(i == 1)
        def _():
            wi.finish_far("p")
            wi.finish_near("2")
            wo[0].start()

        @pl.when(i == 2)
        def _():
            q_fp.wait_recv()
            go(q_push["2"][0])
            q_fm.wait_recv()
            go(q_push["2"][1])
            wi.finish_far("2")
            wo[0].along_y()

        @pl.when(i == 3)
        def _():
            wo[0].along_y2()
            wo[0].forward_z()
            wo[1].start()

        featurize(g)
        scan(g)
        return c

    lax.fori_loop(0, 4, group, 0)

    end_copies = [remote(ends.at[y], ends.at[y], dev(dy=d)) for d in (1, 3, 2)]
    for c in end_copies:
        go(c)
    wo[0].forward_p("2")
    wo[0].forward_m("2")
    wo[1].along_y()
    for c in end_copies:
        c.wait_recv()
    for g in range(4):
        for h in range(2):
            rate = par[g, 24:40, h * 128:(h + 1) * 128]
            hop = jnp.exp(rate * (-1.0 * TEAM))
            total = ends[0, g, h].astype(f32)
            for yy in range(1, 4):
                total = hop * total + ends[yy, g, h].astype(f32)
            totals[ctx, g, h] = total.astype(bf16)
    total_copies = [
        remote(totals.at[ctx], totals.at[ctx], dev(dz=a, dk=b))
        for a in range(4) for b in range(2) if a or b
    ]
    for c in total_copies:
        go(c)
    for name in ("m", "p", "2"):
        wo[0].finish(name)
        go(push_out[name][0])
    wo[1].along_y2()
    wo[1].forward_z()
    for c in total_copies:
        c.wait_recv()

    for g in range(4):
        for h in range(2):
            rate = par[g, 24:40, h * 128:(h + 1) * 128]
            shard_hop = jnp.exp(rate * (-4.0 * TEAM))
            team_hop = jnp.exp(rate * (-1.0 * TEAM))
            v = jnp.zeros((POLES, 128), f32)
            for cc in range(7):
                v = jnp.where(cc < ctx, shard_hop * v + totals[cc, g, h].astype(f32), v)
            for yy in range(3):
                v = jnp.where(yy < y, team_hop * v + ends[yy, g, h].astype(f32), v)
            carry[g, h] = v

    segs = sub.astype(f32)

    def correct(g, c):
        for h in range(2):
            lanes = pl.ds(h * 128, 128)
            rate = par[g, 24:40, lanes]
            power = jnp.exp(-rate)
            wide = lambda v: jnp.broadcast_to(v, (SEGS, 128))
            a = [wide(power[n:n + 1]) for n in range(POLES)]
            begin = carry[g, h]
            states = []
            for n in range(POLES):
                seg_power = jnp.exp(wide(rate[n:n + 1]) * (segs * (-1.0 * STEPS)))
                states.append(pref[g, h, n] + seg_power * wide(begin[n:n + 1]))

            def steps(i, states):
                for u in range(4):
                    at = pl.ds(pl.multiple_of((i * 4 + u) * SEGS, SEGS), SEGS)
                    states = [a[n] * states[n] for n in range(POLES)]
                    gbuf[h, at, :] = q_all[g, h, at, :] * (y_all[g, h, at, :] + tree_sum(states))
                return states

            lax.fori_loop(0, STEPS // 4, steps, states)
            for seg in range(SEGS):
                gated[g, seg * STEPS:(seg + 1) * STEPS, h * 128:(h + 1) * 128] = gbuf[
                    h, pl.ds(seg, STEPS, stride=SEGS), :
                ].astype(bf16)
        return c

    lax.fori_loop(0, 4, correct, 0)

    copy_out.wait()
    wo[1].forward_p("2")
    wo[1].forward_m("2")
    for name in ("m", "p", "2"):
        push_out[name][0].wait_recv()

    def block_rows(who):
        return pl.ds(pl.multiple_of((who % 4) * ROWS, ROWS), ROWS)

    def part_cols(n):
        return pl.ds(pl.multiple_of(n * OUT_COLS, OUT_COLS), OUT_COLS)

    def side_cols(n, side):
        width = OUT_COLS // 2
        return pl.ds(pl.multiple_of(n * OUT_COLS + side * width, width), width)

    def far_copy(n, side):
        width = OUT_COLS // 2
        return pltpu.make_async_remote_copy(
            src_ref=stage.at[block_rows(x + 2), side_cols(n, side)],
            dst_ref=far.at[side, :, pl.ds(pl.multiple_of(n * width, width), width)],
            send_sem=osend.at[side, n], recv_sem=orecv.at[side, n],
            device_id=XM if side else XP, device_id_type=MESH,
        )

    def near_copy(n, side):
        return pltpu.make_async_remote_copy(
            src_ref=stage.at[block_rows(x + (3 if side else 1)), part_cols(n)],
            dst_ref=near.at[side, :, part_cols(n)],
            send_sem=osend.at[2 + side, n], recv_sem=orecv.at[2 + side, n],
            device_id=XM if side else XP, device_id_type=MESH,
        )

    def out_part(n, c):
        cols = part_cols(n)
        acc = jnp.zeros((TEAM, OUT_COLS), f32)
        for g in range(4):
            acc = acc + jnp.dot(gated[g], w_out[g * CH:(g + 1) * CH, cols], preferred_element_type=f32)
        stage[:, cols] = acc.astype(bf16)
        for side in range(2):
            far_copy(n, side).start()
        return c

    def pass_on(n, c):
        width = OUT_COLS // 2
        for side in range(2):
            far_copy(n, side).wait_recv()
            rows, cols = block_rows(x + (3 if side else 1)), side_cols(n, side)
            came = far[side, :, pl.ds(pl.multiple_of(n * width, width), width)]
            stage[rows, cols] = (stage[rows, cols].astype(f32) + came.astype(f32)).astype(bf16)
            near_copy(n, side).start()
        return c

    def add_part(n, c):
        cols = part_cols(n)
        for side in range(2):
            near_copy(n, side).wait_recv()
        total = tok[:, cols].astype(f32) + stage[block_rows(x), cols].astype(f32)
        for side in range(2):
            total = total + near[side, :, cols].astype(f32)
        outv[:, cols] = total.astype(bf16)
        return c

    lax.fori_loop(0, OUT_PARTS // 2, out_part, 0)
    for name in ("m", "p", "2"):
        wo[1].finish(name)
        go(push_out[name][1])
    lax.fori_loop(0, OUT_PARTS // 2, pass_on, 0)
    for name in ("m", "p", "2"):
        push_out[name][1].wait_recv()
    lax.fori_loop(OUT_PARTS // 2, OUT_PARTS, out_part, 0)
    lax.fori_loop(OUT_PARTS // 2, OUT_PARTS, pass_on, 0)
    lax.fori_loop(0, OUT_PARTS, add_part, 0)
    copy_res = pltpu.make_async_copy(outv, out_h, local.at[3])
    copy_res.start()

    def sent_part(n, c):
        for side in range(2):
            far_copy(n, side).wait_send()
            near_copy(n, side).wait_send()
        return c

    lax.fori_loop(0, OUT_PARTS, sent_part, 0)
    for c in started:
        c.wait_send()
    copy_res.wait()


def shards(tokens, norm_gain, w_in, conv_w, decay_rate, residue, skip_gain, w_out):
    anywhere = pl.BlockSpec(memory_space=pl.ANY)
    inside = pl.BlockSpec(memory_space=pltpu.VMEM)
    vmem = pltpu.VMEM
    return pl.pallas_call(
        kernel,
        out_shape=jax.ShapeDtypeStruct(tokens.shape, tokens.dtype),
        in_specs=[anywhere, inside, anywhere, inside, inside, inside, inside, anywhere],
        out_specs=anywhere,
        scratch_shapes=[
            vmem((ROWS, D), bf16),
            vmem((HALO + TEAM, D), bf16),
            vmem((4, 3, D, CH), bf16),
            vmem((4 * CH, D), bf16),
            vmem((4, 64, CH), f32),
            vmem((3, 2, (LEAD + STEPS) * SEGS, 128), f32),
            vmem((2, TEAM, 128), f32),
            vmem((4, 2, TEAM, 128), f32),
            vmem((4, 2, TEAM, 128), f32),
            vmem((4, 2, POLES, SEGS, 128), f32),
            vmem((2, TEAM, 128), f32),
            vmem((4, TEAM, CH), bf16),
            vmem((TEAM, D), bf16),
            vmem((2, ROWS, HALF_COLS), bf16),
            vmem((2, ROWS, D), bf16),
            vmem((4, 4, 2, POLES, 128), bf16),
            vmem((8, 4, 2, POLES, 128), bf16),
            vmem((4, 2, POLES, 128), f32),
            vmem((ROWS, D), bf16),
            pltpu.SemaphoreType.DMA((NSEM,)),
            pltpu.SemaphoreType.DMA((NSEM,)),
            pltpu.SemaphoreType.DMA((4, OUT_PARTS)),
            pltpu.SemaphoreType.DMA((4, OUT_PARTS)),
            pltpu.SemaphoreType.DMA((4,)),
        ],
        compiler_params=pltpu.CompilerParams(
            collective_id=0, has_side_effects=True, vmem_limit_bytes=62 * 1024 * 1024
        ),
    )(
        tokens,
        norm_gain.reshape(1, D),
        jnp.transpose(w_in, (1, 0, 2)),
        jnp.transpose(conv_w, (1, 0, 2)),
        decay_rate,
        residue,
        skip_gain.reshape(1, CH),
        w_out,
    )


def solution(mesh):
    return jax.shard_map(
        shards,
        mesh=mesh,
        in_specs=(
            P(("ctx", "tp"), None),
            P(),
            P(None, None, "tp"),
            P(None, None, "tp"),
            P(None, "tp"),
            P(None, "tp"),
            P("tp"),
            P("tp", None),
        ),
        out_specs=P(("ctx", "tp"), None),
        check_vma=False,
    )
```

```python
import functools

import jax
import jax.numpy as jnp
from jax import lax
from jax.experimental import pallas as pl
from jax.experimental.pallas import tpu as pltpu
from jax.sharding import PartitionSpec as P

TAPS = 7
POLES = 16
D = 4096
CH = 256
ROWS = 128
TEAM = 512
HALO = 16
SEGS = 8
STEPS = TEAM // SEGS
LEAD = 8
EPS = 1e-05
MESH = pl.DeviceIdType.MESH
NSEM = 200
OUT_COLS = 512
OUT_PARTS = D // OUT_COLS
HALF_COLS = D // 2

f32 = jnp.float32
bf16 = jnp.bfloat16


def tree_sum(parts):
    parts = list(parts)
    while len(parts) > 1:
        parts = [
            parts[i] + parts[i + 1] if i + 1 < len(parts) else parts[i]
            for i in range(0, len(parts), 2)
        ]
    return parts[0]


def kernel(
    tok_h, gain, win_h, conv, decay, res, skip, wout_h,
    out_h,
    tok, lhs, w_all, w_out, par, proj, prod, q_all, y_all, pref, gbuf, gated,
    stage, far, near, ends, totals, carry, outv, send, recv, osend, orecv, local,
):
    ctx = lax.axis_index("ctx")
    tp = lax.axis_index("tp")
    z, k = ctx // 2, ctx % 2
    y, x = tp // 4, tp % 4

    def dev(dz=0, dk=0, dy=0, dx=0):
        return (
            ((z + dz) % 4) * 2 + (k + dk) % 2,
            ((y + dy) % 4) * 4 + (x + dx) % 4,
        )

    place = ctx * 4 + y
    after, before = (place + 1) % 32, (place + 31) % 32

    count = [0]
    started = []

    def remote(src, dst, device):
        i = count[0]
        count[0] += 1
        return pltpu.make_async_remote_copy(
            src_ref=src, dst_ref=dst, send_sem=send.at[i], recv_sem=recv.at[i],
            device_id=device, device_id_type=MESH,
        )

    def go(copy):
        copy.start()
        started.append(copy)
        return copy

    gm, gp, g2 = (y + 3) % 4, (y + 1) % 4, (y + 2) % 4

    partners = [dev(dx=1), dev(dx=2), dev(dx=3), dev(dy=1), dev(dy=2), dev(dy=3)]
    partners += [dev(dz=a, dk=b) for a in range(4) for b in range(2) if a or b]
    halo_from = (before // 4, (before % 4) * 4 + 3)
    barrier = pltpu.get_barrier_semaphore()
    for d in partners + [halo_from]:
        pl.semaphore_signal(barrier, inc=1, device_id=d, device_id_type=MESH)

    copy_tok = pltpu.make_async_copy(tok_h, tok, local.at[0])
    copy_win = pltpu.make_async_copy(win_h, w_all.at[y], local.at[1])
    copy_out = pltpu.make_async_copy(
        wout_h, w_out.at[pl.ds(pl.multiple_of(y * CH, CH), CH)], local.at[2]
    )
    copy_tok.start()
    copy_win.start()
    copy_out.start()


    for s in range(3):
        par[y, s * 8:s * 8 + TAPS, :] = conv[s]
    par[y, 24:40, :] = decay[...]
    par[y, 40:56, :] = res[...]
    par[y, 56:57, :] = skip[...]

    def norm_rows(i, c):
        v = tok[pl.ds(pl.multiple_of(i * 16, 16), 16), :].astype(f32)
        ms = jnp.sum(v * v, axis=1, keepdims=True) * (1.0 / D)
        v = (v * lax.rsqrt(ms + EPS) * gain[...]).astype(bf16)
        lhs[pl.ds(pl.multiple_of(HALO + x * ROWS + i * 16, 16), 16), :] = v
        return c

    copy_tok.wait()
    lax.fori_loop(0, ROWS // 16, norm_rows, 0)
    pl.semaphore_wait(barrier, len(partners) + jnp.where(x == 3, 4, 0))

    YP, YM, ZP, ZM, SIB = dev(dy=1), dev(dy=3), dev(dz=1), dev(dz=3), dev(dk=1)
    XP, XM = dev(dx=1), dev(dx=3)

    def share_rows(zz, h):
        return pl.ds(pl.multiple_of(k * 2048 + zz * 512 + h * 256, 256), 256)

    def piece(kind, g, zz, h):
        if kind != "out":
            return w_all.at[g, kind, share_rows(zz, h)]
        at = g * CH + k * 128 + zz * 32 + h * 16
        return w_out.at[pl.ds(pl.multiple_of(at, 16), 16), pl.ds(HALF_COLS, HALF_COLS)]

    def own_piece(kind, h):
        if kind != "out":
            return win_h.at[kind, share_rows(z, h)]
        at = k * 128 + z * 32 + h * 16
        return wout_h.at[pl.ds(pl.multiple_of(at, 16), 16), pl.ds(HALF_COLS, HALF_COLS)]

    class Weights:
        def __init__(self, kind):
            self.kind = kind
            own = lambda h, d: remote(own_piece(kind, h), piece(kind, y, z, h), d)
            self.to_p = [own(h, YP) for h in range(2)]
            self.to_m = [own(h, YM) for h in range(2)]
            self.fwd_p = remote(piece(kind, gm, z, 0), piece(kind, gm, z, 0), YP)
            self.fwd_m = remote(piece(kind, gp, z, 1), piece(kind, gp, z, 1), YM)
            same = lambda g, zz, h, d: remote(piece(kind, g, zz, h), piece(kind, g, zz, h), d)
            self.z_p, self.z_m, self.zf_p, self.zf_m, self.push = {}, {}, {}, {}, {}
            for name, g in (("m", gm), ("p", gp), ("2", g2)):
                self.z_p[name] = [same(g, z, h, ZP) for h in range(2)]
                self.z_m[name] = [same(g, z, h, ZM) for h in range(2)]
                self.zf_p[name] = same(g, (z + 3) % 4, 0, ZP)
                self.zf_m[name] = same(g, (z + 1) % 4, 1, ZM)
                self.push[name] = {}
                if kind != "out":
                    for dz in range(4):
                        for h in range(2):
                            self.push[name][dz, h] = same(g, (z + dz) % 4, h, SIB)

        def start(self):
            go(self.to_p[0])
            go(self.to_m[1])
            go(self.to_p[1])
            go(self.to_m[0])

        def share(self, name, dz, h):
            if self.kind != "out":
                go(self.push[name][dz, h])

        def spread(self, name, h):
            go(self.z_p[name][h])
            go(self.z_m[name][h])
            self.share(name, 0, h)

        def along_y(self):
            self.to_p[0].wait_recv()
            go(self.fwd_p)
            self.spread("m", 0)
            self.to_m[1].wait_recv()
            go(self.fwd_m)
            self.spread("p", 1)
            self.to_p[1].wait_recv()
            self.spread("m", 1)
            self.to_m[0].wait_recv()
            self.spread("p", 0)

        def along_y2(self):
            self.fwd_p.wait_recv()
            self.spread("2", 0)
            self.fwd_m.wait_recv()
            self.spread("2", 1)

        def forward_p(self, name):
            self.z_p[name][0].wait_recv()
            go(self.zf_p[name])
            self.share(name, 3, 0)

        def forward_m(self, name):
            self.z_m[name][1].wait_recv()
            go(self.zf_m[name])
            self.share(name, 1, 1)

        def forward_z(self):
            self.forward_p("m")
            self.forward_m("p")
            self.forward_m("m")
            self.forward_p("p")

        def finish_near(self, name):
            self.z_m[name][0].wait_recv()
            self.share(name, 1, 0)
            self.z_p[name][1].wait_recv()
            self.share(name, 3, 1)

        def finish_far(self, name):
            self.zf_p[name].wait_recv()
            self.share(name, 2, 0)
            self.zf_m[name].wait_recv()
            self.share(name, 2, 1)

        def shared(self, name):
            for c in self.push[name].values():
                c.wait_recv()

        def finish(self, name):
            self.finish_near(name)
            self.finish_far(name)

    def line(kind, g, h):
        if kind != "out":
            return w_all.at[g, kind, pl.ds(pl.multiple_of(k * 2048 + h * 1024, 1024), 1024)]
        at = g * CH + k * 128 + h * 64
        return w_out.at[pl.ds(pl.multiple_of(at, 64), 64), pl.ds(0, HALF_COLS)]

    def own_line(kind, h):
        if kind != "out":
            return win_h.at[kind, pl.ds(pl.multiple_of(k * 2048 + h * 1024, 1024), 1024)]
        at = k * 128 + h * 64
        return wout_h.at[pl.ds(pl.multiple_of(at, 64), 64), pl.ds(0, HALF_COLS)]

    class Lines:
        def __init__(self, kind):
            self.to_p = [remote(own_line(kind, h), line(kind, y, h), YP) for h in range(2)]
            self.to_m = [remote(own_line(kind, h), line(kind, y, h), YM) for h in range(2)]
            same = lambda g, h, d: remote(line(kind, g, h), line(kind, g, h), d)
            self.fwd_p = same(gm, 0, YP)
            self.fwd_m = same(gp, 1, YM)
            self.push = {
                name: [same(g, h, SIB) for h in range(2)]
                for name, g in (("m", gm), ("p", gp), ("2", g2))
            }

        def start_first(self):
            go(self.to_p[0])
            go(self.to_m[1])

        def start_second(self):
            go(self.to_p[1])
            go(self.to_m[0])

        def forward(self):
            self.to_p[0].wait_recv()
            go(self.fwd_p)
            go(self.push["m"][0])
            self.to_m[1].wait_recv()
            go(self.fwd_m)
            go(self.push["p"][1])

        def near(self):
            self.to_p[1].wait_recv()
            go(self.push["m"][1])
            self.to_m[0].wait_recv()
            go(self.push["p"][0])

        def far(self):
            self.fwd_p.wait_recv()
            go(self.push["2"][0])
            self.fwd_m.wait_recv()
            go(self.push["2"][1])

        def shared(self, name):
            for c in self.push[name]:
                c.wait_recv()

    wk, wv, wq = Weights(1), Lines(2), Weights(0)
    wa, wb = Weights("out"), Lines("out")
    push_out = {}
    for name, g in (("m", gm), ("p", gp), ("2", g2)):
        o_half = pl.ds(pl.multiple_of(g * CH + k * 128, 128), 128)
        block = w_out.at[o_half, pl.ds(HALF_COLS, HALF_COLS)]
        push_out[name] = remote(block, block, SIB)

    par_copies = [remote(par.at[y], par.at[y], dev(dy=d)) for d in (1, 3, 2)]

    def x_rows(who, h):
        return lhs.at[pl.ds(pl.multiple_of(HALO + who * ROWS + h * 64, 16), 64)]

    x_p = [remote(x_rows(x, h), x_rows(x, h), XP) for h in range(2)]
    x_m = [remote(x_rows(x, h), x_rows(x, h), XM) for h in range(2)]
    xm, xp = (x + 3) % 4, (x + 1) % 4
    x_fp = remote(x_rows(xm, 0), x_rows(xm, 0), XP)
    x_fm = remote(x_rows(xp, 1), x_rows(xp, 1), XM)
    halo_copies = [
        pltpu.make_async_remote_copy(
            src_ref=lhs.at[pl.ds(TEAM, HALO)], dst_ref=lhs.at[pl.ds(0, HALO)],
            send_sem=send.at[NSEM - 1 - d], recv_sem=recv.at[NSEM - 1],
            device_id=(after // 4, (after % 4) * 4 + d), device_id_type=MESH,
        )
        for d in range(4)
    ]

    @pl.when(x == 3)
    def _():
        for c in halo_copies:
            c.start()

    wk.start()
    go(x_p[0])
    go(x_m[1])
    go(x_p[1])
    go(x_m[0])
    wk.along_y()
    for c in par_copies:
        go(c)
    wq.start()
    wv.start_first()
    wv.start_second()
    x_p[0].wait_recv()
    go(x_fp)
    x_m[1].wait_recv()
    go(x_fm)
    wk.forward_p("m")
    wk.forward_m("p")
    wk.forward_m("m")
    wk.forward_p("p")
    wk.along_y2()
    wq.along_y()
    wv.forward()
    wq.along_y2()
    wk.finish_near("m")
    wk.finish_near("p")
    wk.forward_p("2")
    wk.forward_m("2")
    wk.finish_far("m")
    wk.finish_far("p")
    x_p[1].wait_recv()
    x_m[0].wait_recv()
    x_fp.wait_recv()
    x_fm.wait_recv()
    copy_win.wait()
    halo_copies[0].wait_recv()

    @pl.when(place == 0)
    def _():
        lhs[0:HALO, :] = jnp.zeros((HALO, D), bf16)

    sub = lax.broadcasted_iota(jnp.int32, (SEGS, 128), 0)

    def project(g, streams):
        for s in streams:
            acc = jnp.dot(lhs[...], w_all[g, s], preferred_element_type=f32)
            acc = acc.astype(bf16).astype(f32)
            for h in range(2):
                part = acc[:, h * 128:(h + 1) * 128]
                for seg in range(SEGS):
                    proj[s, h, pl.ds(LEAD * SEGS + seg, STEPS, stride=SEGS), :] = part[
                        HALO + seg * STEPS:HALO + (seg + 1) * STEPS
                    ]
                for j in range(1, TAPS):
                    last = proj[s, h, pl.ds((LEAD + STEPS - j) * SEGS, SEGS), :]
                    first = jnp.broadcast_to(part[HALO - j:HALO - j + 1], (SEGS, 128))
                    proj[s, h, pl.ds((LEAD - j) * SEGS, SEGS), :] = jnp.where(
                        sub == 0, first, pltpu.roll(last, 1, 0)
                    )

    def featurize(g, streams):
        for h in range(2):
            lanes = pl.ds(h * 128, 128)
            taps = [par[g, s * 8:s * 8 + 8, lanes] for s in range(3)]

            def steps(i, c):
                feats = []
                for s in streams:
                    at = pl.multiple_of((i * 8 + LEAD - TAPS + 1) * SEGS, SEGS)
                    rows = proj[s, h, pl.ds(at, 14 * SEGS), :]
                    feats.append(tree_sum([
                        taps[s][j:j + 1] * rows[j * SEGS:j * SEGS + 64] for j in range(TAPS)
                    ]))
                to = pl.ds(pl.multiple_of(i * 64, 64), 64)
                if len(feats) == 2:
                    prod[h, to, :] = feats[0] * feats[1]
                else:
                    q_all[g, h, to, :] = feats[0]
                return c

            lax.fori_loop(0, STEPS // 8, steps, 0)

    def scan(g):
        for h in range(2):
            lanes = pl.ds(h * 128, 128)
            rate = par[g, 24:40, lanes]
            rs = par[g, 40:56, lanes]
            wide = lambda v: jnp.broadcast_to(v, (SEGS, 128))
            power = jnp.exp(-rate)
            a = [wide(power[n:n + 1]) for n in range(POLES)]
            r = [wide(rs[n:n + 1]) for n in range(POLES)]
            direct = wide(par[g, 56:57, lanes])

            def steps(i, states):
                for u in range(4):
                    at = pl.ds(pl.multiple_of((i * 4 + u) * SEGS, SEGS), SEGS)
                    v = prod[h, at, :]
                    states = [a[n] * states[n] + r[n] * v for n in range(POLES)]
                    y_all[g, h, at, :] = tree_sum(states) + direct * v
                return states

            states = lax.fori_loop(
                0, STEPS // 4, steps, [jnp.zeros((SEGS, 128), f32)] * POLES
            )
            last_rows = []
            for n in range(POLES):
                v = states[n]
                for dist in (1, 2, 4):
                    hop = jnp.exp(rate[n:n + 1] * (-1.0 * STEPS * dist))
                    v = v + hop * jnp.where(sub >= dist, pltpu.roll(v, dist, 0), 0.0)
                pref[g, h, n] = jnp.where(sub >= 1, pltpu.roll(v, 1, 0), 0.0)
                last_rows.append(v[SEGS - 1:SEGS])
            ends[y, g, h] = jnp.concatenate(last_rows, axis=0).astype(bf16)

    def group(i, c):
        @pl.when(i == 1)
        def _():
            for c in par_copies:
                c.wait_recv()
            wk.shared("m")
            wv.shared("m")

        @pl.when(i == 2)
        def _():
            wk.shared("p")
            wv.shared("p")

        @pl.when(i == 3)
        def _():
            wk.shared("2")
            wv.shared("2")

        turn = jnp.where(i == 0, 0, jnp.where(i == 1, 3, jnp.where(i == 2, 1, 2)))
        g = (y + turn) % 4
        project(g, (1, 2))

        @pl.when(i == 0)
        def _():
            wk.finish_near("2")
            wk.finish_far("2")
            wv.near()
            wa.start()
            wb.start_first()
            wb.start_second()

        @pl.when(i == 1)
        def _():
            wq.forward_z()

        @pl.when(i == 2)
        def _():
            wv.far()
            wq.finish_near("m")
            wq.finish_near("p")
            wa.along_y()

        @pl.when(i == 3)
        def _():
            wb.forward()
            wq.forward_p("2")
            wq.forward_m("2")
            wq.finish_far("m")
            wq.finish_far("p")
            wa.along_y2()

        featurize(g, (1, 2))
        scan(g)
        return c

    lax.fori_loop(0, 4, group, 0)

    def gate_of(g):
        project(g, (0,))
        featurize(g, (0,))

    end_copies = [remote(ends.at[y], ends.at[y], dev(dy=d)) for d in (1, 3, 2)]
    for c in end_copies:
        go(c)
    gate_of(y)
    for c in end_copies:
        c.wait_recv()
    for g in range(4):
        for h in range(2):
            rate = par[g, 24:40, h * 128:(h + 1) * 128]
            hop = jnp.exp(rate * (-1.0 * TEAM))
            total = ends[0, g, h].astype(f32)
            for yy in range(1, 4):
                total = hop * total + ends[yy, g, h].astype(f32)
            totals[ctx, g, h] = total.astype(bf16)
    total_copies = [
        remote(totals.at[ctx], totals.at[ctx], dev(dz=a, dk=b))
        for a in range(4) for b in range(2) if a or b
    ]
    for c in total_copies:
        go(c)
    wq.shared("m")
    gate_of(gm)
    wq.finish("2")
    wq.shared("p")
    gate_of(gp)
    wa.forward_z()
    wb.near()
    wq.shared("2")
    gate_of(g2)
    for c in total_copies:
        c.wait_recv()

    for g in range(4):
        for h in range(2):
            rate = par[g, 24:40, h * 128:(h + 1) * 128]
            shard_hop = jnp.exp(rate * (-4.0 * TEAM))
            team_hop = jnp.exp(rate * (-1.0 * TEAM))
            v = jnp.zeros((POLES, 128), f32)
            for cc in range(7):
                v = jnp.where(cc < ctx, shard_hop * v + totals[cc, g, h].astype(f32), v)
            for yy in range(3):
                v = jnp.where(yy < y, team_hop * v + ends[yy, g, h].astype(f32), v)
            carry[g, h] = v

    segs = sub.astype(f32)

    def correct(g, c):
        for h in range(2):
            lanes = pl.ds(h * 128, 128)
            rate = par[g, 24:40, lanes]
            power = jnp.exp(-rate)
            wide = lambda v: jnp.broadcast_to(v, (SEGS, 128))
            a = [wide(power[n:n + 1]) for n in range(POLES)]
            begin = carry[g, h]
            states = []
            for n in range(POLES):
                seg_power = jnp.exp(wide(rate[n:n + 1]) * (segs * (-1.0 * STEPS)))
                states.append(pref[g, h, n] + seg_power * wide(begin[n:n + 1]))

            def steps(i, states):
                for u in range(4):
                    at = pl.ds(pl.multiple_of((i * 4 + u) * SEGS, SEGS), SEGS)
                    states = [a[n] * states[n] for n in range(POLES)]
                    gbuf[h, at, :] = q_all[g, h, at, :] * (y_all[g, h, at, :] + tree_sum(states))
                return states

            lax.fori_loop(0, STEPS // 4, steps, states)
            for seg in range(SEGS):
                gated[g, seg * STEPS:(seg + 1) * STEPS, h * 128:(h + 1) * 128] = gbuf[
                    h, pl.ds(seg, STEPS, stride=SEGS), :
                ].astype(bf16)
        return c

    wa.forward_p("2")
    wa.forward_m("2")
    wb.far()
    lax.fori_loop(0, 4, correct, 0)

    copy_out.wait()
    for name in ("m", "p", "2"):
        wb.shared(name)

    def block_rows(who):
        return pl.ds(pl.multiple_of((who % 4) * ROWS, ROWS), ROWS)

    def part_cols(n):
        return pl.ds(pl.multiple_of(n * OUT_COLS, OUT_COLS), OUT_COLS)

    def side_cols(n, side):
        width = OUT_COLS // 2
        return pl.ds(pl.multiple_of(n * OUT_COLS + side * width, width), width)

    def far_copy(n, side):
        width = OUT_COLS // 2
        return pltpu.make_async_remote_copy(
            src_ref=stage.at[block_rows(x + 2), side_cols(n, side)],
            dst_ref=far.at[side, :, pl.ds(pl.multiple_of(n * width, width), width)],
            send_sem=osend.at[side, n], recv_sem=orecv.at[side, n],
            device_id=XM if side else XP, device_id_type=MESH,
        )

    def near_copy(n, side):
        return pltpu.make_async_remote_copy(
            src_ref=stage.at[block_rows(x + (3 if side else 1)), part_cols(n)],
            dst_ref=near.at[side, :, part_cols(n)],
            send_sem=osend.at[2 + side, n], recv_sem=orecv.at[2 + side, n],
            device_id=XM if side else XP, device_id_type=MESH,
        )

    def out_part(n, c):
        cols = part_cols(n)
        acc = jnp.zeros((TEAM, OUT_COLS), f32)
        for g in range(4):
            acc = acc + jnp.dot(gated[g], w_out[g * CH:(g + 1) * CH, cols], preferred_element_type=f32)
        stage[:, cols] = acc.astype(bf16)
        for side in range(2):
            far_copy(n, side).start()
        return c

    def pass_on(n, c):
        width = OUT_COLS // 2
        for side in range(2):
            far_copy(n, side).wait_recv()
            rows, cols = block_rows(x + (3 if side else 1)), side_cols(n, side)
            came = far[side, :, pl.ds(pl.multiple_of(n * width, width), width)]
            stage[rows, cols] = (stage[rows, cols].astype(f32) + came.astype(f32)).astype(bf16)
            near_copy(n, side).start()
        return c

    def add_part(n, c):
        cols = part_cols(n)
        for side in range(2):
            near_copy(n, side).wait_recv()
        total = tok[:, cols].astype(f32) + stage[block_rows(x), cols].astype(f32)
        for side in range(2):
            total = total + near[side, :, cols].astype(f32)
        outv[:, cols] = total.astype(bf16)
        return c

    lax.fori_loop(0, OUT_PARTS // 2, out_part, 0)
    for name in ("m", "p", "2"):
        wa.finish(name)
        go(push_out[name])
    lax.fori_loop(0, OUT_PARTS // 2, pass_on, 0)
    for name in ("m", "p", "2"):
        push_out[name].wait_recv()
    lax.fori_loop(OUT_PARTS // 2, OUT_PARTS, out_part, 0)
    lax.fori_loop(OUT_PARTS // 2, OUT_PARTS, pass_on, 0)
    lax.fori_loop(0, OUT_PARTS, add_part, 0)
    copy_res = pltpu.make_async_copy(outv, out_h, local.at[3])
    copy_res.start()

    def sent_part(n, c):
        for side in range(2):
            far_copy(n, side).wait_send()
            near_copy(n, side).wait_send()
        return c

    lax.fori_loop(0, OUT_PARTS, sent_part, 0)
    @pl.when(x == 3)
    def _():
        for c in halo_copies:
            c.wait_send()

    for c in started:
        c.wait_send()
    copy_res.wait()


def shards(tokens, norm_gain, w_in, conv_w, decay_rate, residue, skip_gain, w_out):
    anywhere = pl.BlockSpec(memory_space=pl.ANY)
    inside = pl.BlockSpec(memory_space=pltpu.VMEM)
    vmem = pltpu.VMEM
    return pl.pallas_call(
        kernel,
        out_shape=jax.ShapeDtypeStruct(tokens.shape, tokens.dtype),
        in_specs=[anywhere, inside, anywhere, inside, inside, inside, inside, anywhere],
        out_specs=anywhere,
        scratch_shapes=[
            vmem((ROWS, D), bf16),
            vmem((HALO + TEAM, D), bf16),
            vmem((4, 3, D, CH), bf16),
            vmem((4 * CH, D), bf16),
            vmem((4, 64, CH), f32),
            vmem((3, 2, (LEAD + STEPS) * SEGS, 128), f32),
            vmem((2, TEAM, 128), f32),
            vmem((4, 2, TEAM, 128), f32),
            vmem((4, 2, TEAM, 128), f32),
            vmem((4, 2, POLES, SEGS, 128), f32),
            vmem((2, TEAM, 128), f32),
            vmem((4, TEAM, CH), bf16),
            vmem((TEAM, D), bf16),
            vmem((2, ROWS, HALF_COLS), bf16),
            vmem((2, ROWS, D), bf16),
            vmem((4, 4, 2, POLES, 128), bf16),
            vmem((8, 4, 2, POLES, 128), bf16),
            vmem((4, 2, POLES, 128), f32),
            vmem((ROWS, D), bf16),
            pltpu.SemaphoreType.DMA((NSEM,)),
            pltpu.SemaphoreType.DMA((NSEM,)),
            pltpu.SemaphoreType.DMA((4, OUT_PARTS)),
            pltpu.SemaphoreType.DMA((4, OUT_PARTS)),
            pltpu.SemaphoreType.DMA((4,)),
        ],
        compiler_params=pltpu.CompilerParams(
            collective_id=0, has_side_effects=True, vmem_limit_bytes=62 * 1024 * 1024
        ),
    )(
        tokens,
        norm_gain.reshape(1, D),
        jnp.transpose(w_in, (1, 0, 2)),
        jnp.transpose(conv_w, (1, 0, 2)),
        decay_rate,
        residue,
        skip_gain.reshape(1, CH),
        w_out,
    )


def solution(mesh):
    return jax.shard_map(
        shards,
        mesh=mesh,
        in_specs=(
            P(("ctx", "tp"), None),
            P(),
            P(None, None, "tp"),
            P(None, None, "tp"),
            P(None, "tp"),
            P(None, "tp"),
            P("tp"),
            P("tp", None),
        ),
        out_specs=P(("ctx", "tp"), None),
        check_vma=False,
    )
```
